128 devices in a mesh: gx: 16 (over x, z), gy: 8 (over y, core).
Axes of the slice: x: 4, y: 4, z: 4, core: 2. Of those that a mesh axis runs over, the one named last changes fastest.
Arguments:
- tokens: bfloat16 [3, 256, 18432], P(None, 'gy', 'gx'), may hold values from -6 to 6
- q_weight: bfloat16 [18432, 12288], P('gx', 'gy'), may hold values from -0.046875 to 0.046875
- kv_weight: bfloat16 [18432, 512], P('gx'), may hold values from -0.046875 to 0.046875
- out_weight: bfloat16 [12288, 18432], P('gy', 'gx'), may hold values from -0.0546875 to 0.0546875
- kv_cache: bfloat16 [256, 8192, 512], P(('gx', 'gy')), may hold values from -92 to 92, as said below
- lengths: int32 [256], P(('gx', 'gy')), may hold values from 1024 to 8189, as said below
Outputs:
- attn_out: bfloat16 [3, 256, 18432], P(None, 'gy', 'gx')
The draws below stay inside these ranges and needn't reach their ends.
Inputs may be any that keep to these rules, and one draw needn't show every extreme that they name: Request r's tokens of step s sit at cache slot lengths[r] + s; some request has the most and some the fewest. `kv_cache`: slots at and beyond a request's length hold stale entries.
All inputs are finite; a program needn't handle non-finite values.
Results may differ from the reference program's by a relative error of at most 0.035.
Values may be sent and summed in bfloat16 or wider, within the bound.
No kernel may reach another device: no remote copies, remote signals or barrier semaphores. Data moves between devices by JAX's collectives and lax.ppermute only.
A program may use at most 256 MiB of HBM per device.

```python
import jax
import jax.numpy as jnp
from jax import lax

D = 18432
HEADS = 48
DH = 256
CTX = 8192
STEPS = 3
REQ = 256
N_GX = 16
N_GY = 8


def draw_kv_cache(key, part):
    key = jax.random.fold_in(key, 11)
    key_base = jax.random.fold_in(key, 0)
    full = jnp.clip(jax.random.normal(key_base, (REQ, CTX, 2 * DH), jnp.float32), -6.0, 6.0)
    return full.astype(jnp.bfloat16)


def draw_lengths(key, part):
    key = jax.random.fold_in(key, 23)
    key_vals, key_perm = jax.random.split(key)
    lowest = CTX // 8
    highest = CTX - STEPS
    values = jax.random.randint(key_vals, (REQ,), lowest, highest + 1)
    order = jax.random.permutation(key_perm, REQ)
    values = values.at[order[0]].set(highest)
    values = values.at[order[1]].set(lowest)
    return values.astype(jnp.int32)


def block_levels(stream_key, extent, cuts, smallest, top_value):
    gain, own = 1.0, jax.random.fold_in(stream_key, 6)
    for axis_at, blocks in cuts:
        steps = jnp.exp(jax.random.uniform(jax.random.fold_in(own, axis_at), (blocks,), jnp.float32, smallest / len(cuts), top_value / len(cuts)))
        gain = gain * jnp.repeat(steps, extent[axis_at] // blocks).reshape([-1 if axis == axis_at else 1 for axis in range(len(extent))])
    return gain


def centred(rng, extent, deviation, limit, cuts=(), kind=jnp.bfloat16):
    values = deviation * jax.random.normal(rng, extent, jnp.float32)
    if cuts:
        values = values * block_levels(rng, extent, cuts, -0.22, 0.18)
    return jnp.clip(values, -limit, limit).astype(kind)


def setup_inputs(seed: int = 0) -> dict:
    splits = jax.random.split(jax.random.key(seed), 7)
    tokens = centred(splits[0], (STEPS, REQ, D), 1.0, 6.0, ((1, 8), (2, 16)))
    q_weight = centred(splits[1], (D, HEADS * DH), D ** -0.5, 0.046875, ((0, 16), (1, 8)))
    kv_weight = centred(splits[2], (D, 2 * DH), D ** -0.5, 0.046875, ((0, 16),))
    out_weight = centred(splits[3], (HEADS * DH, D), (HEADS * DH) ** -0.5, 0.0546875, ((0, 8), (1, 16)))
    kv_cache = draw_kv_cache(jax.random.fold_in(splits[6], 71), 0)
    lengths = draw_lengths(jax.random.fold_in(splits[6], 71), 0)
    return {"tokens": tokens, "q_weight": q_weight, "kv_weight": kv_weight, "out_weight": out_weight, "kv_cache": kv_cache, "lengths": lengths}


def rotate(values, positions):
    head_dim = values.shape[-1]
    half_dim = head_dim // 2
    frequency = 10000.0 ** (-(jnp.arange(half_dim, dtype=jnp.float32) * 2.0 / head_dim))
    angles = positions[..., None] * frequency
    cosine = jnp.cos(angles)
    sine = jnp.sin(angles)
    front_half = values[..., :half_dim]
    back_half = values[..., half_dim:]
    return jnp.concatenate([front_half * cosine - back_half * sine, back_half * cosine + front_half * sine], -1)


def attend_one(arguments):
    queries, store, last_slot = arguments
    keys = store[:, :DH]
    values = store[:, DH:]
    scores = jnp.dot(queries, keys.T, preferred_element_type=jnp.float32) / 16.0
    visible = jnp.arange(CTX, dtype=jnp.int32)[None, :] <= last_slot
    scores = jnp.where(visible, scores, jnp.float32(-1e30))
    top_score = jnp.max(scores, axis=-1, keepdims=True)
    weights = jnp.where(visible, jnp.exp(scores - top_score), jnp.float32(0.0))
    denom = jnp.sum(weights, axis=-1, keepdims=True)
    mixed = jnp.dot(weights.astype(jnp.bfloat16), values, preferred_element_type=jnp.float32)
    return (mixed / denom).astype(jnp.bfloat16)


def place_row(store, new_row, slot):
    return lax.dynamic_update_slice(store, new_row, (slot, jnp.int32(0)))


def reference(tokens, q_weight, kv_weight, out_weight, kv_cache, lengths):
    hidden_cols = HEADS * DH
    joined = jnp.concatenate([q_weight, kv_weight], 1).astype(jnp.float32)
    joined = joined.reshape(N_GX, D // N_GX, hidden_cols + 2 * DH)
    out_blocks = out_weight.astype(jnp.float32).reshape(N_GY, hidden_cols // N_GY, D)
    store_all = kv_cache
    results = []
    for step_index in range(STEPS):
        inputs = tokens[step_index].astype(jnp.float32).reshape(REQ, N_GX, D // N_GX)
        partial_value = jnp.einsum("rgd,gde->gre", inputs, joined)
        partial_value = lax.optimization_barrier(partial_value.astype(jnp.bfloat16)).astype(jnp.float32)
        proj = jnp.sum(partial_value, axis=0)
        slots = (lengths + step_index).astype(jnp.int32)
        pos_float = slots.astype(jnp.float32)
        query_linear = proj[:, :hidden_cols].astype(jnp.bfloat16).reshape(REQ, HEADS, DH)
        queries = rotate(query_linear.astype(jnp.float32), pos_float[:, None]).astype(jnp.bfloat16)
        kv_linear = proj[:, hidden_cols:].astype(jnp.bfloat16)
        new_keys = rotate(kv_linear[:, :DH].astype(jnp.float32), pos_float).astype(jnp.bfloat16)
        new_values = kv_linear[:, DH:]
        new_rows = jnp.concatenate([new_keys, new_values], -1)[:, None, :]
        store_all = jax.vmap(place_row)(store_all, new_rows, slots)
        attended = lax.map(attend_one, (queries, store_all, slots)).reshape(REQ, HEADS * DH)
        head_parts = attended.astype(jnp.float32).reshape(REQ, N_GY, hidden_cols // N_GY)
        out_partial = jnp.einsum("rgh,ghd->grd", head_parts, out_blocks)
        out_partial = lax.optimization_barrier(out_partial.astype(jnp.bfloat16)).astype(jnp.float32)
        results.append(jnp.sum(out_partial, axis=0).astype(jnp.bfloat16))
    return jnp.stack(results)
```

```python
import functools

import jax
import jax.numpy as jnp
from jax import lax
from jax.experimental import pallas as pl
from jax.experimental.pallas import tpu as pltpu
from jax.sharding import PartitionSpec as P

STEPS = 3
LANES = 128
HEAD = 256
SLOT_BLOCK = 1024
MESSAGE = 40
LOG2_E = 1.4426950408889634
VMEM_BYTES = 56 * 1024 * 1024


def across(step_y, step_core):
    count = lax.axis_size("gy")
    ring = count // 2
    return [
        (place, (place // 2 + step_y) % ring * 2 + (place % 2 + step_core) % 2)
        for place in range(count)
    ]


def move(value, step_y, step_core):
    return lax.ppermute(value, "gy", across(step_y, step_core))


def gather_tokens(own):
    half = own.shape[0] // 2
    above = move(own, 1, 0)
    below = move(own, -1, 0)
    other = move(own, 0, 1)
    far_front = move(above[:half], 1, 0)
    far_back = move(below[half:], -1, 0)
    other_above = move(above, 0, 1)
    other_below = move(below, 0, 1)
    far = jnp.concatenate([far_front, far_back], 0)
    other_far = move(far, 0, 1)
    ring = lax.axis_size("gy") // 2
    here = lax.axis_index("gy")
    y, core = here // 2, here % 2
    places = [
        (y + shift) % ring * 2 + (core + flip) % 2
        for shift, flip in [(0, 0), (0, 1), (-1, 0), (1, 0), (-1, 1), (1, 1), (2, 0), (2, 1)]
    ]
    blocks = [own, other, above, below, other_above, other_below, far, other_far]
    return blocks, jnp.stack(places).astype(jnp.int32)


def project_kernel(places, *refs):
    blocks = refs[:8]
    q_weight, kv_weight, out, gathered, spread = refs[8:]
    rows = blocks[0].shape[0]
    requests = rows // STEPS
    for index, block in enumerate(blocks):
        gathered[index * rows : (index + 1) * rows, :] = block[...]
    heads = q_weight.shape[1] // HEAD
    for part in range(heads + 1):
        if part < heads:
            weight = q_weight[:, part * HEAD : (part + 1) * HEAD]
        else:
            weight = kv_weight[...]
        partial = jnp.dot(gathered[...], weight, preferred_element_type=jnp.float32)
        for index in range(8):
            for step in range(STEPS):
                start = index * rows + step * requests
                piece = partial[start : start + requests]
                if part < heads:
                    spots = (step * heads + part, STEPS * heads + step * heads + part)
                else:
                    spots = (2 * STEPS * heads + step,)
                for side, spot in enumerate(spots):
                    spread[pl.ds(index * requests * MESSAGE + spot, requests, stride=MESSAGE), :] = (
                        piece[:, side * LANES : (side + 1) * LANES]
                    )
    for index in range(8):
        size = requests * MESSAGE
        first = pl.multiple_of(places[index] * size, size)
        out[pl.ds(first, size), :] = spread[index * size : (index + 1) * size, :].astype(out.dtype)


def project(places, blocks, q_weight, kv_weight):
    rows = blocks[0].shape[0]
    requests = rows // STEPS * 8
    vmem = pl.BlockSpec(memory_space=pltpu.VMEM)
    return pl.pallas_call(
        project_kernel,
        out_shape=jax.ShapeDtypeStruct((requests * MESSAGE, LANES), jnp.bfloat16),
        in_specs=[pl.BlockSpec(memory_space=pltpu.SMEM)] + [vmem] * 10,
        out_specs=vmem,
        scratch_shapes=[
            pltpu.VMEM((rows * 8, blocks[0].shape[1]), jnp.bfloat16),
            pltpu.VMEM((requests * MESSAGE, LANES), jnp.float32),
        ],
        compiler_params=pltpu.CompilerParams(vmem_limit_bytes=VMEM_BYTES),
        name="project",
    )(places, *blocks, q_weight, kv_weight)


def attend_kernel(lengths, partials, cosine, sine, cache, out, store, summed, query, replies, arrived):
    group = out.shape[1]
    peers = out.shape[0]
    requests, slots, _ = cache.shape
    blocks = slots // SLOT_BLOCK
    heads_rows = (MESSAGE - 4) // 2
    total_rows = group * heads_rows

    def fetch(request, block):
        place = pl.ds(block * SLOT_BLOCK, SLOT_BLOCK)
        return pltpu.make_async_copy(
            cache.at[request, place], store.at[request, place], arrived.at[request, block]
        )

    for block in range(blocks):
        for request in range(requests):

            @pl.when(block * SLOT_BLOCK < lengths[request])
            def _(request=request, block=block):
                fetch(request, block).start()

    for place in range(group):
        total = partials[0, place].astype(jnp.float32)
        for peer in range(1, peers):
            total = total + partials[peer, place].astype(jnp.float32)
        summed[place] = total.astype(jnp.bfloat16).astype(jnp.float32)

    replies[...] = jnp.zeros_like(replies)
    row_step = lax.broadcasted_iota(jnp.int32, (total_rows, LANES), 0) % heads_rows // (heads_rows // STEPS)
    column = lax.broadcasted_iota(jnp.int32, (total_rows, LANES), 1)
    scale = jnp.float32(LOG2_E / 16.0)
    for request in range(requests):
        base = request * MESSAGE
        cos_rows = cosine[request, :heads_rows]
        sin_rows = sine[request, :heads_rows]
        for place in range(group):
            front = summed[place, base : base + heads_rows]
            back = summed[place, base + heads_rows : base + 2 * heads_rows]
            target = pl.ds(place * heads_rows, heads_rows)
            query[target, :LANES] = front * cos_rows - back * sin_rows
            query[target, LANES:] = back * cos_rows + front * sin_rows
        queries = query[...].astype(jnp.bfloat16)

        new = pl.ds(base + 2 * heads_rows, STEPS)
        key_cos = cosine[request, heads_rows : heads_rows + STEPS]
        key_sin = sine[request, heads_rows : heads_rows + STEPS]
        front, back = summed[0, new], summed[group // 4, new]
        new_keys = jnp.concatenate(
            [front * key_cos - back * key_sin, back * key_cos + front * key_sin], -1
        )
        new_values = jnp.concatenate([summed[group // 2, new], summed[3 * group // 4, new]], -1)
        padding = jnp.zeros((LANES - STEPS, HEAD), jnp.float32)
        new_keys = jnp.concatenate([new_keys, padding], 0).astype(jnp.bfloat16)
        new_values = jnp.concatenate([new_values, padding], 0).astype(jnp.bfloat16)

        scores = lax.dot_general(
            queries, new_keys, (((1,), (1,)), ((), ())), preferred_element_type=jnp.float32
        ) * scale
        scores = jnp.where(column <= row_step, scores, jnp.float32(-1e30))
        top = jnp.max(scores, axis=-1, keepdims=True)
        weights = jnp.exp2(scores - top)
        denom = jnp.sum(weights, axis=-1, keepdims=True)
        accum = jnp.dot(weights.astype(jnp.bfloat16), new_values, preferred_element_type=jnp.float32)

        length = lengths[request]

        def one_block(block, state, request=request, queries=queries, length=length):
            top, denom, accum = state
            fetch(request, block).wait()
            place = pl.ds(pl.multiple_of(block * SLOT_BLOCK, SLOT_BLOCK), SLOT_BLOCK)
            keys = store[request, place, :HEAD]
            values = store[request, place, HEAD:]
            slot = block * SLOT_BLOCK + lax.broadcasted_iota(jnp.int32, (1, SLOT_BLOCK), 1)
            hidden = jnp.where(slot < length, jnp.float32(0.0), jnp.float32(-1e30))
            scores = lax.dot_general(
                queries, keys, (((1,), (1,)), ((), ())), preferred_element_type=jnp.float32
            ) * scale + hidden
            new_top = jnp.maximum(top, jnp.max(scores, axis=-1, keepdims=True))
            weights = jnp.exp2(scores - new_top)
            factor = jnp.exp2(top - new_top)
            denom = denom * factor + jnp.sum(weights, axis=-1, keepdims=True)
            accum = accum * factor + jnp.dot(
                weights.astype(jnp.bfloat16), values, preferred_element_type=jnp.float32
            )
            return new_top, denom, accum

        needed = (length + SLOT_BLOCK - 1) // SLOT_BLOCK
        top, denom, accum = lax.fori_loop(0, needed, one_block, (top, denom, accum))
        query[...] = accum / denom
        for place in range(group):
            source = pl.ds(place * heads_rows, heads_rows)
            replies[place, base : base + heads_rows] = query[source, :LANES]
            replies[place, base + heads_rows : base + 2 * heads_rows] = query[source, LANES:]

    for place in range(group):
        reply = replies[place].astype(jnp.bfloat16)
        for peer in range(peers):
            out[peer, place] = reply


def attend(lengths, partials, cosine, sine, cache):
    peers, group, rows, _ = partials.shape
    requests, slots, width = cache.shape
    vmem = pl.BlockSpec(memory_space=pltpu.VMEM)
    return pl.pallas_call(
        attend_kernel,
        out_shape=jax.ShapeDtypeStruct(partials.shape, jnp.bfloat16),
        in_specs=[
            pl.BlockSpec(memory_space=pltpu.SMEM),
            vmem,
            vmem,
            vmem,
            pl.BlockSpec(memory_space=pl.ANY),
        ],
        out_specs=vmem,
        scratch_shapes=[
            pltpu.VMEM((requests, slots, width), jnp.bfloat16),
            pltpu.VMEM((group, rows, LANES), jnp.float32),
            pltpu.VMEM((group * (MESSAGE - 4) // 2, HEAD), jnp.float32),
            pltpu.VMEM((group, rows, LANES), jnp.float32),
            pltpu.SemaphoreType.DMA((requests, slots // SLOT_BLOCK)),
        ],
        compiler_params=pltpu.CompilerParams(vmem_limit_bytes=VMEM_BYTES),
        name="attend",
    )(lengths, partials, cosine, sine, cache)


def output_kernel(places, attended, out_weight, out, spread, rows_ref):
    blocks, rows, width = out.shape
    requests = rows // STEPS
    heads = out_weight.shape[0] // HEAD
    size = requests * MESSAGE
    for index in range(blocks):
        first = pl.multiple_of(places[index] * size, size)
        spread[...] = attended[pl.ds(first, size), :].astype(jnp.float32)
        for step in range(STEPS):
            for head in range(heads):
                for side in range(2):
                    spot = side * STEPS * heads + step * heads + head
                    lane = head * HEAD + side * LANES
                    start = index * rows + step * requests
                    rows_ref[start : start + requests, lane : lane + LANES] = spread[
                        pl.ds(spot, requests, stride=MESSAGE), :
                    ].astype(jnp.bfloat16)
    for first in range(0, width, HEAD):
        size = min(HEAD, width - first)
        partial = jnp.dot(
            rows_ref[...], out_weight[:, first : first + size], preferred_element_type=jnp.float32
        ).astype(jnp.bfloat16)
        for index in range(blocks):
            out[index, :, first : first + size] = partial[index * rows : (index + 1) * rows]


def output_partial(places, attended, out_weight, rows):
    blocks = places.shape[0]
    vmem = pl.BlockSpec(memory_space=pltpu.VMEM)
    return pl.pallas_call(
        output_kernel,
        out_shape=jax.ShapeDtypeStruct((blocks, rows, out_weight.shape[1]), jnp.bfloat16),
        in_specs=[pl.BlockSpec(memory_space=pltpu.SMEM), vmem, vmem],
        out_specs=vmem,
        scratch_shapes=[
            pltpu.VMEM((rows // STEPS * MESSAGE, LANES), jnp.float32),
            pltpu.VMEM((blocks * rows, out_weight.shape[0]), jnp.bfloat16),
        ],
        compiler_params=pltpu.CompilerParams(vmem_limit_bytes=VMEM_BYTES),
        name="output",
    )(places, attended, out_weight)


def plus(first, second):
    return (first.astype(jnp.float32) + second.astype(jnp.float32)).astype(jnp.bfloat16)


def per_device(tokens, q_weight, kv_weight, out_weight, kv_cache, lengths):
    gx_count, gy_count = lax.axis_size("gx"), lax.axis_size("gy")
    here = lax.axis_index("gy")
    y, core = here // 2, here % 2
    ring = gy_count // 2
    steps, block_requests, depth = tokens.shape
    rows = steps * block_requests
    req_local = kv_cache.shape[0]
    heads_local = q_weight.shape[1] // HEAD
    kv_columns = kv_weight.shape[1] // ring

    own_kv = lax.dynamic_slice_in_dim(kv_weight, y * kv_columns, kv_columns, 1)
    positions = (lengths[:, None] + jnp.arange(STEPS, dtype=jnp.int32)[None, :]).astype(jnp.float32)
    half = HEAD // 2
    frequency = 10000.0 ** (-(jnp.arange(half, dtype=jnp.float32) * 2.0 / HEAD))
    angles = positions[..., None] * frequency

    def table(values):
        per_head = jnp.repeat(values, heads_local, axis=1)
        filler = jnp.zeros((req_local, 24 - STEPS - STEPS * heads_local, half), jnp.float32)
        return jnp.concatenate([per_head, values, filler], 1)

    cosine, sine = table(jnp.cos(angles)), table(jnp.sin(angles))

    blocks, places = gather_tokens(tokens.reshape(rows, depth))
    sent = project(places, blocks, q_weight, own_kv)
    everywhere = ("gx", "gy")
    sent = sent.reshape(gx_count * gy_count, req_local * MESSAGE, LANES)
    partials = lax.all_to_all(sent, everywhere, split_axis=0, concat_axis=0, tiled=True)
    partials = partials.reshape(gx_count, gy_count, req_local * MESSAGE, LANES)
    attended = attend(lengths, partials, cosine, sine, kv_cache)
    attended = attended.reshape(gx_count * gy_count, req_local * MESSAGE, LANES)
    attended = lax.all_to_all(attended, everywhere, split_axis=0, concat_axis=0, tiled=True)
    attended = attended.reshape(-1, LANES)

    shifts = jnp.arange(ring, dtype=jnp.int32)
    ahead = (y + shifts) % ring * 2
    for_other = output_partial(ahead + 1 - core, attended, out_weight, rows)
    from_other = move(for_other, 0, 1)
    mine = output_partial(ahead + core, attended, out_weight, rows)
    mine = plus(mine, from_other)
    cut = rows // 2
    front = move(mine[2, :cut], 1, 0)
    back = move(mine[2, cut:], -1, 0)
    up = jnp.concatenate([plus(mine[1, :cut], front), mine[1, cut:]], 0)
    down = jnp.concatenate([mine[3, :cut], plus(mine[3, cut:], back)], 0)
    from_below = move(up, 1, 0)
    from_above = move(down, -1, 0)
    result = (
        mine[0].astype(jnp.float32)
        + from_below.astype(jnp.float32)
        + from_above.astype(jnp.float32)
    ).astype(jnp.bfloat16)
    return result.reshape(steps, block_requests, -1)


def solution(mesh):
    in_specs = (
        P(None, "gy", "gx"),
        P("gx", "gy"),
        P("gx", None),
        P("gy", "gx"),
        P(("gx", "gy"), None, None),
        P(("gx", "gy")),
    )
    out_specs = P(None, "gy", "gx")
    return jax.shard_map(
        per_device, mesh=mesh, in_specs=in_specs, out_specs=out_specs, check_vma=False
    )
```

```python
import functools

import jax
import jax.numpy as jnp
from jax import lax
from jax.experimental import pallas as pl
from jax.experimental.pallas import tpu as pltpu
from jax.sharding import PartitionSpec as P

STEPS = 3
LANES = 128
HEAD = 256
SLOT_BLOCK = 4096
MESSAGE = 40
REPLY = 36
LOG2_E = 1.4426950408889634
PROJECT_VMEM = 56 * 1024 * 1024
ATTEND_VMEM = 60 * 1024 * 1024
OUTPUT_VMEM = 24 * 1024 * 1024


def across(step_y, step_core):
    count = lax.axis_size("gy")
    ring = count // 2
    return [
        (place, (place // 2 + step_y) % ring * 2 + (place % 2 + step_core) % 2)
        for place in range(count)
    ]


def move(value, step_y, step_core):
    return lax.ppermute(value, "gy", across(step_y, step_core))


def gather_and_project(own, q_weight, kv_weight, peers):
    half = own.shape[0] // 2
    ring = lax.axis_size("gy") // 2
    here = lax.axis_index("gy")
    y, core = here // 2, here % 2

    def places(*steps):
        return jnp.stack(
            [(y + shift) % ring * 2 + (core + flip) % 2 for shift, flip in steps]
        ).astype(jnp.int32)

    above = move(own, 1, 0)
    below = move(own, -1, 0)
    other = move(own, 0, 1)
    far_front = move(above[:half], 1, 0)
    far_back = move(below[half:], -1, 0)
    other_above = move(above, 0, 1)
    other_below = move(below, 0, 1)
    first = places((0, 0), (0, 1), (-1, 0), (1, 0))
    sent = project(first, [own, other, above, below], q_weight, kv_weight, peers)
    far = jnp.concatenate([far_front, far_back], 0)
    far, sent = lax.optimization_barrier((far, sent))
    other_far = move(far, 0, 1)
    second = places((-1, 1), (1, 1), (2, 0), (2, 1))
    blocks = [other_above, other_below, far, other_far]
    return project(second, blocks, q_weight, kv_weight, peers, sent)


def project_kernel(count, places, *refs):
    blocks = refs[:count]
    q_weight, kv_weight = refs[count : count + 2]
    out, gathered, spread, narrow, sent = refs[-5:]
    rows = blocks[0].shape[0]
    requests = rows // STEPS
    heads = q_weight.shape[1] // HEAD
    for index, block in enumerate(blocks):
        gathered[index * rows : (index + 1) * rows, :] = block[...]
    for part in range(heads + 1):
        if part < heads:
            weight = q_weight[:, part * HEAD : (part + 1) * HEAD]
        else:
            weight = kv_weight[...]
        partial = jnp.dot(gathered[...], weight, preferred_element_type=jnp.float32)
        for index in range(count):
            for step in range(STEPS):
                start = index * rows + step * requests
                piece = partial[start : start + requests]
                if part < heads:
                    spots = (step * heads + part, STEPS * heads + step * heads + part)
                else:
                    spots = (2 * STEPS * heads + step,)
                for side, spot in enumerate(spots):
                    spread[pl.ds(index * requests * MESSAGE + spot, requests, stride=MESSAGE), :] = (
                        piece[:, side * LANES : (side + 1) * LANES]
                    )
    size = requests * MESSAGE
    copies = []
    for index in range(count):
        here = pl.ds(index * size, size)
        narrow[here, :] = spread[here, :].astype(narrow.dtype)
        first = pl.multiple_of(places[index] * size, size)
        copies.append(
            pltpu.make_async_copy(narrow.at[here], out.at[pl.ds(first, size)], sent.at[index])
        )
        copies[-1].start()
    for copy in copies:
        copy.wait()


def project(places, blocks, q_weight, kv_weight, peers, written=None):
    count = len(blocks)
    rows, depth = blocks[0].shape
    requests = rows // STEPS
    held = requests * count * MESSAGE
    vmem = pl.BlockSpec(memory_space=pltpu.VMEM)
    in_specs = [pl.BlockSpec(memory_space=pltpu.SMEM)] + [vmem] * (count + 2)
    operands = [places, *blocks, q_weight, kv_weight]
    if written is not None:
        in_specs.append(pl.BlockSpec(memory_space=pltpu.HBM))
        operands.append(written)
    return pl.pallas_call(
        functools.partial(project_kernel, count),
        out_shape=jax.ShapeDtypeStruct((requests * peers * MESSAGE, LANES), jnp.bfloat16),
        in_specs=in_specs,
        out_specs=pl.BlockSpec(memory_space=pltpu.HBM),
        input_output_aliases={} if written is None else {len(operands) - 1: 0},
        scratch_shapes=[
            pltpu.VMEM((rows * count, depth), jnp.bfloat16),
            pltpu.VMEM((held, LANES), jnp.float32),
            pltpu.VMEM((held, LANES), jnp.bfloat16),
            pltpu.SemaphoreType.DMA((count,)),
        ],
        compiler_params=pltpu.CompilerParams(vmem_limit_bytes=PROJECT_VMEM),
        name="project",
    )(*operands)


def attend_kernel(
    lengths, partials, cosine, sine, cache, out, keys, values, summed, query, replies, narrow, score,
    arrived, sent
):
    peers, group, _, _ = partials.shape
    requests, slots, _ = cache.shape
    blocks = slots // SLOT_BLOCK
    heads_rows = REPLY // 2
    rows = group * heads_rows
    scale = jnp.float32(LOG2_E / 16.0)

    def fetch(request, side, block):
        place = pl.ds(pl.multiple_of(block * SLOT_BLOCK, SLOT_BLOCK), SLOT_BLOCK)
        return pltpu.make_async_copy(
            cache.at[request, place, pl.ds(side * HEAD, HEAD)],
            (keys, values)[side].at[request, place],
            arrived.at[request, side, block],
        )

    def start(request, side):
        if request < requests:
            for block in range(blocks):
                fetch(request, side, block).start()

    start(0, 0)
    for place in range(group):
        total = partials[0, place].astype(jnp.float32)
        for peer in range(1, peers):
            total = total + partials[peer, place].astype(jnp.float32)
        summed[place] = total.astype(jnp.bfloat16).astype(jnp.float32)

    start(1, 0)
    start(0, 1)
    row_step = lax.broadcasted_iota(jnp.int32, (rows, LANES), 0) % heads_rows // (heads_rows // STEPS)
    column = lax.broadcasted_iota(jnp.int32, (rows, LANES), 1)

    def prepare(request):
        base = request * MESSAGE
        cos_rows = cosine[request, :heads_rows]
        sin_rows = sine[request, :heads_rows]
        for place in range(group):
            front = summed[place, base : base + heads_rows]
            back = summed[place, base + heads_rows : base + 2 * heads_rows]
            target = pl.ds(place * heads_rows, heads_rows)
            query[request, target, :LANES] = front * cos_rows - back * sin_rows
            query[request, target, LANES:] = back * cos_rows + front * sin_rows
        queries = query[request].astype(jnp.bfloat16)
        new = pl.ds(base + 2 * heads_rows, STEPS)
        key_cos = cosine[request, heads_rows : heads_rows + STEPS]
        key_sin = sine[request, heads_rows : heads_rows + STEPS]
        front, back = summed[0, new], summed[group // 4, new]
        new_keys = jnp.concatenate(
            [front * key_cos - back * key_sin, back * key_cos + front * key_sin], -1
        )
        new_values = jnp.concatenate([summed[group // 2, new], summed[3 * group // 4, new]], -1)
        padding = jnp.zeros((LANES - STEPS, HEAD), jnp.float32)
        new_keys = jnp.concatenate([new_keys, padding], 0).astype(jnp.bfloat16)
        new_values = jnp.concatenate([new_values, padding], 0).astype(jnp.bfloat16)
        scores = lax.dot_general(
            queries, new_keys, (((1,), (1,)), ((), ())), preferred_element_type=jnp.float32
        )
        return queries, jnp.where(column <= row_step, scores, jnp.float32(-1e30)), new_values

    def score_block(request, queries, block, top):
        place = pl.ds(pl.multiple_of(block * SLOT_BLOCK, SLOT_BLOCK), SLOT_BLOCK)
        fetch(request, 0, block).wait()
        slot = block * SLOT_BLOCK + lax.broadcasted_iota(jnp.int32, (1, SLOT_BLOCK), 1)
        hidden = jnp.where(slot < lengths[request], jnp.float32(0.0), jnp.float32(-1e30))
        scores = hidden + lax.dot_general(
            queries, keys[request, place], (((1,), (1,)), ((), ())), preferred_element_type=jnp.float32
        )
        score[request, block] = scores
        for lane in range(0, SLOT_BLOCK, LANES):
            top = jnp.maximum(top, scores[:, lane : lane + LANES])
        return top

    def begin(new_scores, new_values, top):
        top = jnp.max(top, axis=-1, keepdims=True) * scale
        weights = jnp.exp2(new_scores * scale - top)
        mixed = jnp.dot(weights.astype(jnp.bfloat16), new_values, preferred_element_type=jnp.float32)
        return top, weights, mixed

    def mix_block(request, top, block, denom, accum):
        place = pl.ds(pl.multiple_of(block * SLOT_BLOCK, SLOT_BLOCK), SLOT_BLOCK)
        fetch(request, 1, block).wait()
        weights = jnp.exp2(score[request, block] * scale - top)
        for lane in range(0, SLOT_BLOCK, LANES):
            denom = denom + weights[:, lane : lane + LANES]
        accum = accum + jnp.dot(
            weights.astype(jnp.bfloat16), values[request, place], preferred_element_type=jnp.float32
        )
        return denom, accum

    def finish(request, denom, accum):
        query[request] = accum / jnp.sum(denom, axis=-1, keepdims=True)
        for place in range(group):
            base = (place * requests + request) * REPLY
            source = pl.ds(place * heads_rows, heads_rows)
            replies[base : base + heads_rows] = query[request, source, :LANES]
            replies[base + heads_rows : base + 2 * heads_rows] = query[request, source, LANES:]

    ready = [prepare(request) for request in range(requests)]
    queries, new_scores, _ = ready[0]
    top = lax.fori_loop(
        0, blocks, functools.partial(score_block, 0, queries), new_scores
    )
    for request in range(requests):
        _, new_scores, new_values = ready[request]
        top, denom, accum = begin(new_scores, new_values, top)
        start(request + 1, 1)
        start(request + 2, 0)
        if request + 1 < requests:
            following, following_scores, _ = ready[request + 1]

            def both(block, state, request=request, top=top, following=following):
                next_top, denom, accum = state
                next_top = score_block(request + 1, following, block, next_top)
                denom, accum = mix_block(request, top, block, denom, accum)
                return next_top, denom, accum

            top, denom, accum = lax.fori_loop(
                0, blocks, both, (following_scores, denom, accum)
            )
        else:

            def last(block, state, request=request, top=top):
                return mix_block(request, top, block, *state)

            denom, accum = lax.fori_loop(0, blocks, last, (denom, accum))
        finish(request, denom, accum)

    narrow[...] = replies[...].astype(jnp.bfloat16)
    copies = [pltpu.make_async_copy(narrow, out.at[peer], sent.at[peer]) for peer in range(peers)]
    for copy in copies:
        copy.start()
    for copy in copies:
        copy.wait()


def attend(lengths, partials, cosine, sine, cache):
    peers, group, rows, _ = partials.shape
    requests, slots, _ = cache.shape
    blocks = slots // SLOT_BLOCK
    query_rows = group * REPLY // 2
    reply_rows = group * requests * REPLY
    vmem = pl.BlockSpec(memory_space=pltpu.VMEM)
    hbm = pl.BlockSpec(memory_space=pltpu.HBM)
    return pl.pallas_call(
        attend_kernel,
        out_shape=jax.ShapeDtypeStruct((peers, reply_rows, LANES), jnp.bfloat16),
        in_specs=[pl.BlockSpec(memory_space=pltpu.SMEM), vmem, vmem, vmem, hbm],
        out_specs=hbm,
        scratch_shapes=[
            pltpu.VMEM((requests, slots, HEAD), jnp.bfloat16),
            pltpu.VMEM((requests, slots, HEAD), jnp.bfloat16),
            pltpu.VMEM((group, rows, LANES), jnp.float32),
            pltpu.VMEM((requests, query_rows, HEAD), jnp.float32),
            pltpu.VMEM((reply_rows, LANES), jnp.float32),
            pltpu.VMEM((reply_rows, LANES), jnp.bfloat16),
            pltpu.VMEM((requests, blocks, query_rows, SLOT_BLOCK), jnp.float32),
            pltpu.SemaphoreType.DMA((requests, 2, blocks)),
            pltpu.SemaphoreType.DMA((peers,)),
        ],
        compiler_params=pltpu.CompilerParams(vmem_limit_bytes=ATTEND_VMEM),
        name="attend",
    )(lengths, partials, cosine, sine, cache)


def output_kernel(places, attended, out_weight, out, spread, rows_ref):
    blocks, rows, width = out.shape
    requests = rows // STEPS
    heads = out_weight.shape[0] // HEAD
    size = requests * REPLY
    for index in range(blocks):
        first = pl.multiple_of(places[index] * size, size)
        spread[...] = attended[pl.ds(first, size), :].astype(jnp.float32)
        for step in range(STEPS):
            for head in range(heads):
                for side in range(2):
                    spot = side * STEPS * heads + step * heads + head
                    lane = head * HEAD + side * LANES
                    start = index * rows + step * requests
                    rows_ref[start : start + requests, lane : lane + LANES] = spread[
                        pl.ds(spot, requests, stride=REPLY), :
                    ].astype(jnp.bfloat16)
    for first in range(0, width, HEAD):
        size = min(HEAD, width - first)
        partial = jnp.dot(
            rows_ref[...], out_weight[:, first : first + size], preferred_element_type=jnp.float32
        ).astype(jnp.bfloat16)
        for index in range(blocks):
            out[index, :, first : first + size] = partial[index * rows : (index + 1) * rows]


def output_partial(places, attended, out_weight, rows):
    blocks = places.shape[0]
    vmem = pl.BlockSpec(memory_space=pltpu.VMEM)
    return pl.pallas_call(
        output_kernel,
        out_shape=jax.ShapeDtypeStruct((blocks, rows, out_weight.shape[1]), jnp.bfloat16),
        in_specs=[pl.BlockSpec(memory_space=pltpu.SMEM), vmem, vmem],
        out_specs=vmem,
        scratch_shapes=[
            pltpu.VMEM((rows // STEPS * REPLY, LANES), jnp.float32),
            pltpu.VMEM((blocks * rows, out_weight.shape[0]), jnp.bfloat16),
        ],
        compiler_params=pltpu.CompilerParams(vmem_limit_bytes=OUTPUT_VMEM),
        name="output",
    )(places, attended, out_weight)


def plus(first, second):
    return (first.astype(jnp.float32) + second.astype(jnp.float32)).astype(jnp.bfloat16)


def per_device(tokens, q_weight, kv_weight, out_weight, kv_cache, lengths):
    gx_count, gy_count = lax.axis_size("gx"), lax.axis_size("gy")
    here = lax.axis_index("gy")
    y, core = here // 2, here % 2
    ring = gy_count // 2
    steps, block_requests, depth = tokens.shape
    rows = steps * block_requests
    req_local = kv_cache.shape[0]
    heads_local = q_weight.shape[1] // HEAD
    kv_columns = kv_weight.shape[1] // ring

    own_kv = lax.dynamic_slice_in_dim(kv_weight, y * kv_columns, kv_columns, 1)
    positions = (lengths[:, None] + jnp.arange(STEPS, dtype=jnp.int32)[None, :]).astype(jnp.float32)
    half = HEAD // 2
    frequency = 10000.0 ** (-(jnp.arange(half, dtype=jnp.float32) * 2.0 / HEAD))
    angles = positions[..., None] * frequency

    def table(values):
        per_head = jnp.repeat(values, heads_local, axis=1)
        filler = jnp.zeros((req_local, 24 - STEPS - STEPS * heads_local, half), jnp.float32)
        return jnp.concatenate([per_head, values, filler], 1)

    cosine, sine = table(jnp.cos(angles)), table(jnp.sin(angles))

    peers = gx_count * gy_count * req_local // block_requests
    sent = gather_and_project(tokens.reshape(rows, depth), q_weight, own_kv, peers)
    everywhere = ("gx", "gy")
    sent = sent.reshape(gx_count * gy_count, req_local * MESSAGE, LANES)
    partials = lax.all_to_all(sent, everywhere, split_axis=0, concat_axis=0, tiled=True)
    partials = partials.reshape(gx_count, gy_count, req_local * MESSAGE, LANES)
    attended = attend(lengths, partials, cosine, sine, kv_cache)
    attended = attended.reshape(gx_count * gy_count, req_local * REPLY, LANES)
    attended = lax.all_to_all(attended, everywhere, split_axis=0, concat_axis=0, tiled=True)
    attended = attended.reshape(-1, LANES)

    shifts = jnp.arange(ring, dtype=jnp.int32)
    ahead = (y + shifts) % ring * 2
    for_other = output_partial(ahead + 1 - core, attended, out_weight, rows)
    from_other = move(for_other, 0, 1)
    mine = output_partial(ahead + core, attended, out_weight, rows)
    mine = plus(mine, from_other)
    cut = rows // 2
    front = move(mine[2, :cut], 1, 0)
    back = move(mine[2, cut:], -1, 0)
    up = jnp.concatenate([plus(mine[1, :cut], front), mine[1, cut:]], 0)
    down = jnp.concatenate([mine[3, :cut], plus(mine[3, cut:], back)], 0)
    from_below = move(up, 1, 0)
    from_above = move(down, -1, 0)
    result = (
        mine[0].astype(jnp.float32)
        + from_below.astype(jnp.float32)
        + from_above.astype(jnp.float32)
    ).astype(jnp.bfloat16)
    return result.reshape(steps, block_requests, -1)


def solution(mesh):
    in_specs = (
        P(None, "gy", "gx"),
        P("gx", "gy"),
        P("gx", None),
        P("gy", "gx"),
        P(("gx", "gy"), None, None),
        P(("gx", "gy")),
    )
    out_specs = P(None, "gy", "gx")
    return jax.shard_map(
        per_device, mesh=mesh, in_specs=in_specs, out_specs=out_specs, check_vma=False
    )
```

```python
import functools

import jax
import jax.numpy as jnp
from jax import lax
from jax.experimental import pallas as pl
from jax.experimental.pallas import tpu as pltpu
from jax.sharding import PartitionSpec as P

STEPS = 3
LANES = 128
HEAD = 256
SLOT_BLOCK = 4096
MESSAGE = 40
REPLY = 36
LOG2_E = 1.4426950408889634
PROJECT_VMEM = 53 * 1024 * 1024
ATTEND_VMEM = 60 * 1024 * 1024
OUTPUT_VMEM = 24 * 1024 * 1024


def across(step_y, step_core):
    count = lax.axis_size("gy")
    ring = count // 2
    return [
        (place, (place // 2 + step_y) % ring * 2 + (place % 2 + step_core) % 2)
        for place in range(count)
    ]


def move(value, step_y, step_core):
    return lax.ppermute(value, "gy", across(step_y, step_core))


def gather_and_project(own, q_weight, kv_weight, peers):
    half = own.shape[0] // 2
    ring = lax.axis_size("gy") // 2
    here = lax.axis_index("gy")
    y, core = here // 2, here % 2

    def places(*steps):
        return jnp.stack(
            [(y + shift) % ring * 2 + (core + flip) % 2 for shift, flip in steps]
        ).astype(jnp.int32)

    above = move(own, 1, 0)
    below = move(own, -1, 0)
    other = move(own, 0, 1)
    far_front = move(above[:half], 1, 0)
    far_back = move(below[half:], -1, 0)
    other_above = move(above, 0, 1)
    other_below = move(below, 0, 1)
    first = places((0, 0), (0, 1), (-1, 0), (1, 0))
    sent = project(first, [own, other, above, below], q_weight, kv_weight, peers)
    far = jnp.concatenate([far_front, far_back], 0)
    far, sent = lax.optimization_barrier((far, sent))
    other_far = move(far, 0, 1)
    second = places((-1, 1), (1, 1), (2, 0), (2, 1))
    blocks = [other_above, other_below, far, other_far]
    return project(second, blocks, q_weight, kv_weight, peers, sent)


def project_kernel(count, places, *refs):
    blocks = refs[:count]
    q_weight, kv_weight = refs[count : count + 2]
    out, gathered, spread, narrow, sent = refs[-5:]
    rows = blocks[0].shape[0]
    requests = rows // STEPS
    heads = q_weight.shape[1] // HEAD
    for index, block in enumerate(blocks):
        gathered[index * rows : (index + 1) * rows, :] = block[...]
    for part in range(heads + 1):
        if part < heads:
            weight = q_weight[:, part * HEAD : (part + 1) * HEAD]
        else:
            weight = kv_weight[...]
        partial = jnp.dot(gathered[...], weight, preferred_element_type=jnp.float32)
        for index in range(count):
            for step in range(STEPS):
                start = index * rows + step * requests
                piece = partial[start : start + requests]
                if part < heads:
                    spots = (step * heads + part, STEPS * heads + step * heads + part)
                else:
                    spots = (2 * STEPS * heads + step,)
                for side, spot in enumerate(spots):
                    spread[pl.ds(index * requests * MESSAGE + spot, requests, stride=MESSAGE), :] = (
                        piece[:, side * LANES : (side + 1) * LANES]
                    )
    size = requests * MESSAGE
    copies = []
    for index in range(count):
        here = pl.ds(index * size, size)
        narrow[here, :] = spread[here, :].astype(narrow.dtype)
        first = pl.multiple_of(places[index] * size, size)
        copies.append(
            pltpu.make_async_copy(narrow.at[here], out.at[pl.ds(first, size)], sent.at[index])
        )
        copies[-1].start()
    for copy in copies:
        copy.wait()


def project(places, blocks, q_weight, kv_weight, peers, written=None):
    count = len(blocks)
    rows, depth = blocks[0].shape
    requests = rows // STEPS
    held = requests * count * MESSAGE
    vmem = pl.BlockSpec(memory_space=pltpu.VMEM)
    in_specs = [pl.BlockSpec(memory_space=pltpu.SMEM)] + [vmem] * (count + 2)
    operands = [places, *blocks, q_weight, kv_weight]
    if written is not None:
        in_specs.append(pl.BlockSpec(memory_space=pltpu.HBM))
        operands.append(written)
    return pl.pallas_call(
        functools.partial(project_kernel, count),
        out_shape=jax.ShapeDtypeStruct((requests * peers * MESSAGE, LANES), jnp.bfloat16),
        in_specs=in_specs,
        out_specs=pl.BlockSpec(memory_space=pltpu.HBM),
        input_output_aliases={} if written is None else {len(operands) - 1: 0},
        scratch_shapes=[
            pltpu.VMEM((rows * count, depth), jnp.bfloat16),
            pltpu.VMEM((held, LANES), jnp.float32),
            pltpu.VMEM((held, LANES), jnp.bfloat16),
            pltpu.SemaphoreType.DMA((count,)),
        ],
        compiler_params=pltpu.CompilerParams(vmem_limit_bytes=PROJECT_VMEM),
        name="project",
    )(*operands)


def attend_kernel(
    lengths, partials, cosine, sine, cached_keys, cache, out, keys, values, summed, query, replies, narrow,
    score, arrived, sent
):
    peers, group, _, _ = partials.shape
    requests, slots, _ = cache.shape
    blocks = slots // SLOT_BLOCK
    heads_rows = REPLY // 2
    rows = group * heads_rows
    scale = jnp.float32(LOG2_E / 16.0)

    def fetch(request, side, block):
        place = pl.ds(pl.multiple_of(block * SLOT_BLOCK, SLOT_BLOCK), SLOT_BLOCK)
        if side == 0:
            source, target = cached_keys.at[request, :, place], keys.at[request, :, place]
        else:
            source = cache.at[request, place, pl.ds(HEAD, HEAD)]
            target = values.at[request, place]
        return pltpu.make_async_copy(source, target, arrived.at[request, side, block])

    def start(request, side):
        if request < requests:
            for block in range(blocks):
                fetch(request, side, block).start()

    start(0, 0)
    for place in range(group):
        total = partials[0, place].astype(jnp.float32)
        for peer in range(1, peers):
            total = total + partials[peer, place].astype(jnp.float32)
        summed[place] = total.astype(jnp.bfloat16).astype(jnp.float32)

    start(0, 1)
    row_step = lax.broadcasted_iota(jnp.int32, (rows, LANES), 0) % heads_rows // (heads_rows // STEPS)
    column = lax.broadcasted_iota(jnp.int32, (rows, LANES), 1)

    def prepare(request):
        base = request * MESSAGE
        cos_rows = cosine[request, :heads_rows]
        sin_rows = sine[request, :heads_rows]
        for place in range(group):
            front = summed[place, base : base + heads_rows]
            back = summed[place, base + heads_rows : base + 2 * heads_rows]
            target = pl.ds(place * heads_rows, heads_rows)
            query[request, target, :LANES] = front * cos_rows - back * sin_rows
            query[request, target, LANES:] = back * cos_rows + front * sin_rows
        queries = query[request].astype(jnp.bfloat16)
        new = pl.ds(base + 2 * heads_rows, STEPS)
        key_cos = cosine[request, heads_rows : heads_rows + STEPS]
        key_sin = sine[request, heads_rows : heads_rows + STEPS]
        front, back = summed[0, new], summed[group // 4, new]
        new_keys = jnp.concatenate(
            [front * key_cos - back * key_sin, back * key_cos + front * key_sin], -1
        )
        new_values = jnp.concatenate([summed[group // 2, new], summed[3 * group // 4, new]], -1)
        padding = jnp.zeros((LANES - STEPS, HEAD), jnp.float32)
        new_keys = jnp.concatenate([new_keys, padding], 0).astype(jnp.bfloat16)
        new_values = jnp.concatenate([new_values, padding], 0).astype(jnp.bfloat16)
        scores = lax.dot_general(
            queries, new_keys, (((1,), (1,)), ((), ())), preferred_element_type=jnp.float32
        )
        return queries, jnp.where(column <= row_step, scores, jnp.float32(-1e30)), new_values

    def score_block(request, queries, block, top):
        place = pl.ds(pl.multiple_of(block * SLOT_BLOCK, SLOT_BLOCK), SLOT_BLOCK)
        fetch(request, 0, block).wait()
        slot = block * SLOT_BLOCK + lax.broadcasted_iota(jnp.int32, (1, SLOT_BLOCK), 1)
        hidden = jnp.where(slot < lengths[request], jnp.float32(0.0), jnp.float32(-1e30))
        scores = hidden + jnp.dot(
            queries, keys[request, :, place], preferred_element_type=jnp.float32
        )
        score[request, block] = scores
        for lane in range(0, SLOT_BLOCK, LANES):
            top = jnp.maximum(top, scores[:, lane : lane + LANES])
        return top

    def begin(new_scores, new_values, top):
        top = jnp.max(top, axis=-1, keepdims=True) * scale
        weights = jnp.exp2(new_scores * scale - top)
        mixed = jnp.dot(weights.astype(jnp.bfloat16), new_values, preferred_element_type=jnp.float32)
        return top, weights, mixed

    def mix_block(request, top, block, denom, accum):
        place = pl.ds(pl.multiple_of(block * SLOT_BLOCK, SLOT_BLOCK), SLOT_BLOCK)
        fetch(request, 1, block).wait()
        weights = jnp.exp2(score[request, block] * scale - top)
        for lane in range(0, SLOT_BLOCK, LANES):
            denom = denom + weights[:, lane : lane + LANES]
        accum = accum + jnp.dot(
            weights.astype(jnp.bfloat16), values[request, place], preferred_element_type=jnp.float32
        )
        return denom, accum

    def finish(request, denom, accum):
        query[request] = accum / jnp.sum(denom, axis=-1, keepdims=True)
        for place in range(group):
            base = (place * requests + request) * REPLY
            source = pl.ds(place * heads_rows, heads_rows)
            replies[base : base + heads_rows] = query[request, source, :LANES]
            replies[base + heads_rows : base + 2 * heads_rows] = query[request, source, LANES:]

    ready = [prepare(request) for request in range(requests)]
    for request in range(requests):
        queries, new_scores, new_values = ready[request]
        start(request + 1, 0)
        top = lax.fori_loop(
            0, blocks, functools.partial(score_block, request, queries), new_scores
        )
        start(request + 1, 1)
        top, denom, accum = begin(new_scores, new_values, top)

        def mix(block, state, request=request, top=top):
            return mix_block(request, top, block, *state)

        denom, accum = lax.fori_loop(0, blocks, mix, (denom, accum))
        finish(request, denom, accum)

    narrow[...] = replies[...].astype(jnp.bfloat16)
    copies = [pltpu.make_async_copy(narrow, out.at[peer], sent.at[peer]) for peer in range(peers)]
    for copy in copies:
        copy.start()
    for copy in copies:
        copy.wait()


def attend(lengths, partials, cosine, sine, cached_keys, cache):
    peers, group, rows, _ = partials.shape
    requests, slots, _ = cache.shape
    blocks = slots // SLOT_BLOCK
    query_rows = group * REPLY // 2
    reply_rows = group * requests * REPLY
    vmem = pl.BlockSpec(memory_space=pltpu.VMEM)
    hbm = pl.BlockSpec(memory_space=pltpu.HBM)
    return pl.pallas_call(
        attend_kernel,
        out_shape=jax.ShapeDtypeStruct((peers, reply_rows, LANES), jnp.bfloat16),
        in_specs=[pl.BlockSpec(memory_space=pltpu.SMEM), vmem, vmem, vmem, hbm, hbm],
        out_specs=hbm,
        scratch_shapes=[
            pltpu.VMEM((requests, HEAD, slots), jnp.bfloat16),
            pltpu.VMEM((requests, slots, HEAD), jnp.bfloat16),
            pltpu.VMEM((group, rows, LANES), jnp.float32),
            pltpu.VMEM((requests, query_rows, HEAD), jnp.float32),
            pltpu.VMEM((reply_rows, LANES), jnp.float32),
            pltpu.VMEM((reply_rows, LANES), jnp.bfloat16),
            pltpu.VMEM((requests, blocks, query_rows, SLOT_BLOCK), jnp.float32),
            pltpu.SemaphoreType.DMA((requests, 2, blocks)),
            pltpu.SemaphoreType.DMA((peers,)),
        ],
        compiler_params=pltpu.CompilerParams(vmem_limit_bytes=ATTEND_VMEM),
        name="attend",
    )(lengths, partials, cosine, sine, cached_keys, cache)


def arrange_kernel(places, attended, out, spread):
    blocks = places.shape[0]
    size = spread.shape[0]
    requests = size // REPLY
    rows = requests * STEPS
    heads = out.shape[1] // HEAD
    for index in range(blocks):
        first = pl.multiple_of(places[index] * size, size)
        spread[...] = attended[pl.ds(first, size), :].astype(jnp.float32)
        for step in range(STEPS):
            for head in range(heads):
                for side in range(2):
                    spot = side * STEPS * heads + step * heads + head
                    lane = head * HEAD + side * LANES
                    start = index * rows + step * requests
                    out[start : start + requests, lane : lane + LANES] = spread[
                        pl.ds(spot, requests, stride=REPLY), :
                    ].astype(jnp.bfloat16)


def arrange(places, attended, rows, depth):
    vmem = pl.BlockSpec(memory_space=pltpu.VMEM)
    return pl.pallas_call(
        arrange_kernel,
        out_shape=jax.ShapeDtypeStruct((places.shape[0] * rows, depth), jnp.bfloat16),
        in_specs=[pl.BlockSpec(memory_space=pltpu.SMEM), vmem],
        out_specs=vmem,
        scratch_shapes=[pltpu.VMEM((rows // STEPS * REPLY, LANES), jnp.float32)],
        compiler_params=pltpu.CompilerParams(vmem_limit_bytes=OUTPUT_VMEM),
        name="arrange",
    )(places, attended)


def output_kernel(half, arranged, out_weight, out):
    blocks, rows, width = out.shape
    taken = pl.ds(half * blocks * rows, blocks * rows)
    for first in range(0, width, HEAD):
        size = min(HEAD, width - first)
        partial = jnp.dot(
            arranged[taken, :], out_weight[:, first : first + size], preferred_element_type=jnp.float32
        ).astype(jnp.bfloat16)
        for index in range(blocks):
            out[index, :, first : first + size] = partial[index * rows : (index + 1) * rows]


def output_partial(half, arranged, out_weight, rows):
    blocks = arranged.shape[0] // rows // 2
    vmem = pl.BlockSpec(memory_space=pltpu.VMEM)
    return pl.pallas_call(
        functools.partial(output_kernel, half),
        out_shape=jax.ShapeDtypeStruct((blocks, rows, out_weight.shape[1]), jnp.bfloat16),
        in_specs=[vmem, vmem],
        out_specs=vmem,
        compiler_params=pltpu.CompilerParams(vmem_limit_bytes=OUTPUT_VMEM),
        name="output",
    )(arranged, out_weight)


def plus(first, second):
    return (first.astype(jnp.float32) + second.astype(jnp.float32)).astype(jnp.bfloat16)


def per_device(tokens, q_weight, kv_weight, out_weight, kv_cache, lengths):
    gx_count, gy_count = lax.axis_size("gx"), lax.axis_size("gy")
    here = lax.axis_index("gy")
    y, core = here // 2, here % 2
    ring = gy_count // 2
    steps, block_requests, depth = tokens.shape
    rows = steps * block_requests
    req_local = kv_cache.shape[0]
    heads_local = q_weight.shape[1] // HEAD
    kv_columns = kv_weight.shape[1] // ring

    own_kv = lax.dynamic_slice_in_dim(kv_weight, y * kv_columns, kv_columns, 1)
    positions = (lengths[:, None] + jnp.arange(STEPS, dtype=jnp.int32)[None, :]).astype(jnp.float32)
    half = HEAD // 2
    frequency = 10000.0 ** (-(jnp.arange(half, dtype=jnp.float32) * 2.0 / HEAD))
    angles = positions[..., None] * frequency

    def table(values):
        per_head = jnp.repeat(values, heads_local, axis=1)
        filler = jnp.zeros((req_local, 24 - STEPS - STEPS * heads_local, half), jnp.float32)
        return jnp.concatenate([per_head, values, filler], 1)

    cosine, sine = table(jnp.cos(angles)), table(jnp.sin(angles))

    peers = gx_count * gy_count * req_local // block_requests
    sent = gather_and_project(tokens.reshape(rows, depth), q_weight, own_kv, peers)
    everywhere = ("gx", "gy")
    sent = sent.reshape(gx_count * gy_count, req_local * MESSAGE, LANES)
    partials = lax.all_to_all(sent, everywhere, split_axis=0, concat_axis=0, tiled=True)
    partials = partials.reshape(gx_count, gy_count, req_local * MESSAGE, LANES)
    cached_keys = jnp.swapaxes(kv_cache[:, :, :HEAD], 1, 2)
    attended = attend(lengths, partials, cosine, sine, cached_keys, kv_cache)
    attended = attended.reshape(gx_count * gy_count, req_local * REPLY, LANES)
    attended = lax.all_to_all(attended, everywhere, split_axis=0, concat_axis=0, tiled=True)
    attended = attended.reshape(-1, LANES)

    shifts = jnp.arange(ring, dtype=jnp.int32)
    ahead = (y + shifts) % ring * 2
    order = jnp.concatenate([ahead + 1 - core, ahead + core])
    arranged = arrange(order, attended, rows, out_weight.shape[0])
    for_other = output_partial(0, arranged, out_weight, rows)
    from_other = move(for_other, 0, 1)
    mine = output_partial(1, arranged, out_weight, rows)
    mine = plus(mine, from_other)
    cut = rows // 2
    front = move(mine[2, :cut], 1, 0)
    back = move(mine[2, cut:], -1, 0)
    from_below = move(mine[1], 1, 0)
    from_above = move(mine[3], -1, 0)
    far = jnp.concatenate([move(front, 1, 0), move(back, -1, 0)], 0)
    terms = [mine[0], from_below, from_above, far]
    result = sum(term.astype(jnp.float32) for term in terms).astype(jnp.bfloat16)
    return result.reshape(steps, block_requests, -1)


def solution(mesh):
    in_specs = (
        P(None, "gy", "gx"),
        P("gx", "gy"),
        P("gx", None),
        P("gy", "gx"),
        P(("gx", "gy"), None, None),
        P(("gx", "gy")),
    )
    out_specs = P(None, "gy", "gx")
    return jax.shard_map(
        per_device, mesh=mesh, in_specs=in_specs, out_specs=out_specs, check_vma=False
    )
```

```python
import functools

import jax
import jax.numpy as jnp
from jax import lax
from jax.experimental import pallas as pl
from jax.experimental.pallas import tpu as pltpu
from jax.sharding import PartitionSpec as P

STEPS = 3
LANES = 128
HEAD = 256
SLOT_BLOCK = 4096
MESSAGE = 40
REPLY = 36
LOG2_E = 1.4426950408889634
PROJECT_VMEM = 53 * 1024 * 1024
ATTEND_VMEM = 60 * 1024 * 1024
OUTPUT_VMEM = 24 * 1024 * 1024


def across(step_y, step_core):
    count = lax.axis_size("gy")
    ring = count // 2
    return [
        (place, (place // 2 + step_y) % ring * 2 + (place % 2 + step_core) % 2)
        for place in range(count)
    ]


def move(value, step_y, step_core):
    return lax.ppermute(value, "gy", across(step_y, step_core))


def gather_and_project(own, q_weight, kv_weight, peers):
    half = own.shape[0] // 2
    ring = lax.axis_size("gy") // 2
    here = lax.axis_index("gy")
    y, core = here // 2, here % 2

    def places(*steps):
        return jnp.stack(
            [(y + shift) % ring * 2 + (core + flip) % 2 for shift, flip in steps]
        ).astype(jnp.int32)

    above = move(own, 1, 0)
    below = move(own, -1, 0)
    other = move(own, 0, 1)
    far_front = move(above[:half], 1, 0)
    far_back = move(below[half:], -1, 0)
    other_above = move(above, 0, 1)
    other_below = move(below, 0, 1)
    first = places((0, 0), (0, 1), (-1, 0), (1, 0))
    sent = project(first, [own, other, above, below], q_weight, kv_weight, peers)
    far = jnp.concatenate([far_front, far_back], 0)
    far, sent = lax.optimization_barrier((far, sent))
    other_far = move(far, 0, 1)
    second = places((-1, 1), (1, 1), (2, 0), (2, 1))
    blocks = [other_above, other_below, far, other_far]
    return project(second, blocks, q_weight, kv_weight, peers, sent)


def project_kernel(count, places, *refs):
    blocks = refs[:count]
    q_weight, kv_weight = refs[count : count + 2]
    out, gathered, spread, narrow, sent = refs[-5:]
    rows = blocks[0].shape[0]
    requests = rows // STEPS
    heads = q_weight.shape[1] // HEAD
    for index, block in enumerate(blocks):
        gathered[index * rows : (index + 1) * rows, :] = block[...]
    for part in range(heads + 1):
        if part < heads:
            weight = q_weight[:, part * HEAD : (part + 1) * HEAD]
        else:
            weight = kv_weight[...]
        partial = jnp.dot(gathered[...], weight, preferred_element_type=jnp.float32)
        for index in range(count):
            for step in range(STEPS):
                start = index * rows + step * requests
                piece = partial[start : start + requests]
                if part < heads:
                    spots = (step * heads + part, STEPS * heads + step * heads + part)
                else:
                    spots = (2 * STEPS * heads + step,)
                for side, spot in enumerate(spots):
                    spread[pl.ds(index * requests * MESSAGE + spot, requests, stride=MESSAGE), :] = (
                        piece[:, side * LANES : (side + 1) * LANES]
                    )
    size = requests * MESSAGE
    copies = []
    for index in range(count):
        here = pl.ds(index * size, size)
        narrow[here, :] = spread[here, :].astype(narrow.dtype)
        first = pl.multiple_of(places[index] * size, size)
        copies.append(
            pltpu.make_async_copy(narrow.at[here], out.at[pl.ds(first, size)], sent.at[index])
        )
        copies[-1].start()
    for copy in copies:
        copy.wait()


def project(places, blocks, q_weight, kv_weight, peers, written=None):
    count = len(blocks)
    rows, depth = blocks[0].shape
    requests = rows // STEPS
    held = requests * count * MESSAGE
    vmem = pl.BlockSpec(memory_space=pltpu.VMEM)
    in_specs = [pl.BlockSpec(memory_space=pltpu.SMEM)] + [vmem] * (count + 2)
    operands = [places, *blocks, q_weight, kv_weight]
    if written is not None:
        in_specs.append(pl.BlockSpec(memory_space=pltpu.HBM))
        operands.append(written)
    return pl.pallas_call(
        functools.partial(project_kernel, count),
        out_shape=jax.ShapeDtypeStruct((requests * peers * MESSAGE, LANES), jnp.bfloat16),
        in_specs=in_specs,
        out_specs=pl.BlockSpec(memory_space=pltpu.HBM),
        input_output_aliases={} if written is None else {len(operands) - 1: 0},
        scratch_shapes=[
            pltpu.VMEM((rows * count, depth), jnp.bfloat16),
            pltpu.VMEM((held, LANES), jnp.float32),
            pltpu.VMEM((held, LANES), jnp.bfloat16),
            pltpu.SemaphoreType.DMA((count,)),
        ],
        compiler_params=pltpu.CompilerParams(vmem_limit_bytes=PROJECT_VMEM),
        name="project",
    )(*operands)


def transpose_kernel(cache, out):
    out[0] = cache[0].T


def transpose_keys(cache):
    requests, slots, _ = cache.shape
    rows = 1024
    return pl.pallas_call(
        transpose_kernel,
        grid=(requests, slots // rows),
        out_shape=jax.ShapeDtypeStruct((requests, HEAD, slots), cache.dtype),
        in_specs=[pl.BlockSpec((1, rows, HEAD), lambda request, block: (request, block, 0))],
        out_specs=pl.BlockSpec((1, HEAD, rows), lambda request, block: (request, 0, block)),
        compiler_params=pltpu.CompilerParams(vmem_limit_bytes=ATTEND_VMEM),
        name="transpose_keys",
    )(cache)


def attend_kernel(
    lengths, partials, cosine, sine, cached_keys, cache, out, keys, values, summed, query, replies, narrow,
    score, arrived, sent
):
    peers, group, _, _ = partials.shape
    requests, slots, _ = cache.shape
    blocks = slots // SLOT_BLOCK
    heads_rows = REPLY // 2
    rows = group * heads_rows
    scale = jnp.float32(LOG2_E / 16.0)

    def fetch(request, side, block):
        place = pl.ds(pl.multiple_of(block * SLOT_BLOCK, SLOT_BLOCK), SLOT_BLOCK)
        if side == 0:
            source, target = cached_keys.at[request, :, place], keys.at[request, :, place]
        else:
            source = cache.at[request, place, pl.ds(HEAD, HEAD)]
            target = values.at[request, place]
        return pltpu.make_async_copy(source, target, arrived.at[request, side, block])

    def start(request, side):
        if request < requests:
            for block in range(blocks):
                fetch(request, side, block).start()

    start(0, 0)
    for place in range(group):
        total = partials[0, place].astype(jnp.float32)
        for peer in range(1, peers):
            total = total + partials[peer, place].astype(jnp.float32)
        summed[place] = total.astype(jnp.bfloat16).astype(jnp.float32)

    start(0, 1)
    row_step = lax.broadcasted_iota(jnp.int32, (rows, LANES), 0) % heads_rows // (heads_rows // STEPS)
    column = lax.broadcasted_iota(jnp.int32, (rows, LANES), 1)

    def prepare(request):
        base = request * MESSAGE
        cos_rows = cosine[request, :heads_rows]
        sin_rows = sine[request, :heads_rows]
        for place in range(group):
            front = summed[place, base : base + heads_rows]
            back = summed[place, base + heads_rows : base + 2 * heads_rows]
            target = pl.ds(place * heads_rows, heads_rows)
            query[request, target, :LANES] = front * cos_rows - back * sin_rows
            query[request, target, LANES:] = back * cos_rows + front * sin_rows
        queries = query[request].astype(jnp.bfloat16)
        new = pl.ds(base + 2 * heads_rows, STEPS)
        key_cos = cosine[request, heads_rows : heads_rows + STEPS]
        key_sin = sine[request, heads_rows : heads_rows + STEPS]
        front, back = summed[0, new], summed[group // 4, new]
        new_keys = jnp.concatenate(
            [front * key_cos - back * key_sin, back * key_cos + front * key_sin], -1
        )
        new_values = jnp.concatenate([summed[group // 2, new], summed[3 * group // 4, new]], -1)
        padding = jnp.zeros((LANES - STEPS, HEAD), jnp.float32)
        new_keys = jnp.concatenate([new_keys, padding], 0).astype(jnp.bfloat16)
        new_values = jnp.concatenate([new_values, padding], 0).astype(jnp.bfloat16)
        scores = lax.dot_general(
            queries, new_keys, (((1,), (1,)), ((), ())), preferred_element_type=jnp.float32
        )
        return queries, jnp.where(column <= row_step, scores, jnp.float32(-1e30)), new_values

    def score_block(request, queries, block, top):
        place = pl.ds(pl.multiple_of(block * SLOT_BLOCK, SLOT_BLOCK), SLOT_BLOCK)
        fetch(request, 0, block).wait()
        slot = block * SLOT_BLOCK + lax.broadcasted_iota(jnp.int32, (1, SLOT_BLOCK), 1)
        hidden = jnp.where(slot < lengths[request], jnp.float32(0.0), jnp.float32(-1e30))
        scores = hidden + jnp.dot(
            queries, keys[request, :, place], preferred_element_type=jnp.float32
        )
        score[request, block] = scores
        for lane in range(0, SLOT_BLOCK, LANES):
            top = jnp.maximum(top, scores[:, lane : lane + LANES])
        return top

    def begin(new_scores, new_values, top):
        top = jnp.max(top, axis=-1, keepdims=True) * scale
        weights = jnp.exp2(new_scores * scale - top)
        mixed = jnp.dot(weights.astype(jnp.bfloat16), new_values, preferred_element_type=jnp.float32)
        return top, weights, mixed

    def mix_block(request, top, block, denom, accum):
        place = pl.ds(pl.multiple_of(block * SLOT_BLOCK, SLOT_BLOCK), SLOT_BLOCK)
        fetch(request, 1, block).wait()
        weights = jnp.exp2(score[request, block] * scale - top)
        for lane in range(0, SLOT_BLOCK, LANES):
            denom = denom + weights[:, lane : lane + LANES]
        accum = accum + jnp.dot(
            weights.astype(jnp.bfloat16), values[request, place], preferred_element_type=jnp.float32
        )
        return denom, accum

    def finish(request, denom, accum):
        query[request] = accum / jnp.sum(denom, axis=-1, keepdims=True)
        for place in range(group):
            base = (place * requests + request) * REPLY
            source = pl.ds(place * heads_rows, heads_rows)
            replies[base : base + heads_rows] = query[request, source, :LANES]
            replies[base + heads_rows : base + 2 * heads_rows] = query[request, source, LANES:]

    ready = [prepare(request) for request in range(requests)]
    for request in range(requests):
        queries, new_scores, new_values = ready[request]
        start(request + 1, 0)
        top = lax.fori_loop(
            0, blocks, functools.partial(score_block, request, queries), new_scores
        )
        start(request + 1, 1)
        top, denom, accum = begin(new_scores, new_values, top)

        def mix(block, state, request=request, top=top):
            return mix_block(request, top, block, *state)

        denom, accum = lax.fori_loop(0, blocks, mix, (denom, accum))
        finish(request, denom, accum)

    narrow[...] = replies[...].astype(jnp.bfloat16)
    copies = [pltpu.make_async_copy(narrow, out.at[peer], sent.at[peer]) for peer in range(peers)]
    for copy in copies:
        copy.start()
    for copy in copies:
        copy.wait()


def attend(lengths, partials, cosine, sine, cached_keys, cache):
    peers, group, rows, _ = partials.shape
    requests, slots, _ = cache.shape
    blocks = slots // SLOT_BLOCK
    query_rows = group * REPLY // 2
    reply_rows = group * requests * REPLY
    vmem = pl.BlockSpec(memory_space=pltpu.VMEM)
    hbm = pl.BlockSpec(memory_space=pltpu.HBM)
    return pl.pallas_call(
        attend_kernel,
        out_shape=jax.ShapeDtypeStruct((peers, reply_rows, LANES), jnp.bfloat16),
        in_specs=[pl.BlockSpec(memory_space=pltpu.SMEM), vmem, vmem, vmem, hbm, hbm],
        out_specs=hbm,
        scratch_shapes=[
            pltpu.VMEM((requests, HEAD, slots), jnp.bfloat16),
            pltpu.VMEM((requests, slots, HEAD), jnp.bfloat16),
            pltpu.VMEM((group, rows, LANES), jnp.float32),
            pltpu.VMEM((requests, query_rows, HEAD), jnp.float32),
            pltpu.VMEM((reply_rows, LANES), jnp.float32),
            pltpu.VMEM((reply_rows, LANES), jnp.bfloat16),
            pltpu.VMEM((requests, blocks, query_rows, SLOT_BLOCK), jnp.float32),
            pltpu.SemaphoreType.DMA((requests, 2, blocks)),
            pltpu.SemaphoreType.DMA((peers,)),
        ],
        compiler_params=pltpu.CompilerParams(vmem_limit_bytes=ATTEND_VMEM),
        name="attend",
    )(lengths, partials, cosine, sine, cached_keys, cache)


def arrange_kernel(places, attended, out, spread):
    blocks = places.shape[0]
    size = spread.shape[0]
    requests = size // REPLY
    rows = requests * STEPS
    heads = out.shape[1] // HEAD
    for index in range(blocks):
        first = pl.multiple_of(places[index] * size, size)
        spread[...] = attended[pl.ds(first, size), :].astype(jnp.float32)
        for step in range(STEPS):
            for head in range(heads):
                for side in range(2):
                    spot = side * STEPS * heads + step * heads + head
                    lane = head * HEAD + side * LANES
                    start = index * rows + step * requests
                    out[start : start + requests, lane : lane + LANES] = spread[
                        pl.ds(spot, requests, stride=REPLY), :
                    ].astype(jnp.bfloat16)


def arrange(places, attended, rows, depth):
    vmem = pl.BlockSpec(memory_space=pltpu.VMEM)
    return pl.pallas_call(
        arrange_kernel,
        out_shape=jax.ShapeDtypeStruct((places.shape[0] * rows, depth), jnp.bfloat16),
        in_specs=[pl.BlockSpec(memory_space=pltpu.SMEM), vmem],
        out_specs=vmem,
        scratch_shapes=[pltpu.VMEM((rows // STEPS * REPLY, LANES), jnp.float32)],
        compiler_params=pltpu.CompilerParams(vmem_limit_bytes=OUTPUT_VMEM),
        name="arrange",
    )(places, attended)


def output_kernel(half, arranged, out_weight, out):
    blocks, rows, width = out.shape
    taken = pl.ds(half * blocks * rows, blocks * rows)
    for first in range(0, width, HEAD):
        size = min(HEAD, width - first)
        partial = jnp.dot(
            arranged[taken, :], out_weight[:, first : first + size], preferred_element_type=jnp.float32
        ).astype(jnp.bfloat16)
        for index in range(blocks):
            out[index, :, first : first + size] = partial[index * rows : (index + 1) * rows]


def output_partial(half, arranged, out_weight, rows):
    blocks = arranged.shape[0] // rows // 2
    vmem = pl.BlockSpec(memory_space=pltpu.VMEM)
    return pl.pallas_call(
        functools.partial(output_kernel, half),
        out_shape=jax.ShapeDtypeStruct((blocks, rows, out_weight.shape[1]), jnp.bfloat16),
        in_specs=[vmem, vmem],
        out_specs=vmem,
        compiler_params=pltpu.CompilerParams(vmem_limit_bytes=OUTPUT_VMEM),
        name="output",
    )(arranged, out_weight)


def plus(first, second):
    return (first.astype(jnp.float32) + second.astype(jnp.float32)).astype(jnp.bfloat16)


def per_device(tokens, q_weight, kv_weight, out_weight, kv_cache, lengths):
    gx_count, gy_count = lax.axis_size("gx"), lax.axis_size("gy")
    here = lax.axis_index("gy")
    y, core = here // 2, here % 2
    ring = gy_count // 2
    steps, block_requests, depth = tokens.shape
    rows = steps * block_requests
    req_local = kv_cache.shape[0]
    heads_local = q_weight.shape[1] // HEAD
    kv_columns = kv_weight.shape[1] // ring

    own_kv = lax.dynamic_slice_in_dim(kv_weight, y * kv_columns, kv_columns, 1)
    positions = (lengths[:, None] + jnp.arange(STEPS, dtype=jnp.int32)[None, :]).astype(jnp.float32)
    half = HEAD // 2
    frequency = 10000.0 ** (-(jnp.arange(half, dtype=jnp.float32) * 2.0 / HEAD))
    angles = positions[..., None] * frequency

    def table(values):
        per_head = jnp.repeat(values, heads_local, axis=1)
        filler = jnp.zeros((req_local, 24 - STEPS - STEPS * heads_local, half), jnp.float32)
        return jnp.concatenate([per_head, values, filler], 1)

    cosine, sine = table(jnp.cos(angles)), table(jnp.sin(angles))

    peers = gx_count * gy_count * req_local // block_requests
    sent = gather_and_project(tokens.reshape(rows, depth), q_weight, own_kv, peers)
    everywhere = ("gx", "gy")
    sent = sent.reshape(gx_count * gy_count, req_local * MESSAGE, LANES)
    partials = lax.all_to_all(sent, everywhere, split_axis=0, concat_axis=0, tiled=True)
    partials = partials.reshape(gx_count, gy_count, req_local * MESSAGE, LANES)
    cached_keys = transpose_keys(kv_cache)
    attended = attend(lengths, partials, cosine, sine, cached_keys, kv_cache)
    attended = attended.reshape(gx_count * gy_count, req_local * REPLY, LANES)
    attended = lax.all_to_all(attended, everywhere, split_axis=0, concat_axis=0, tiled=True)
    attended = attended.reshape(-1, LANES)

    shifts = jnp.arange(ring, dtype=jnp.int32)
    ahead = (y + shifts) % ring * 2
    order = jnp.concatenate([ahead + 1 - core, ahead + core])
    arranged = arrange(order, attended, rows, out_weight.shape[0])
    for_other = output_partial(0, arranged, out_weight, rows)
    from_other = move(for_other, 0, 1)
    mine = output_partial(1, arranged, out_weight, rows)
    mine = plus(mine, from_other)
    cut = rows // 2
    front = move(mine[2, :cut], 1, 0)
    back = move(mine[2, cut:], -1, 0)
    from_below = move(mine[1], 1, 0)
    from_above = move(mine[3], -1, 0)
    far = jnp.concatenate([move(front, 1, 0), move(back, -1, 0)], 0)
    terms = [mine[0], from_below, from_above, far]
    result = sum(term.astype(jnp.float32) for term in terms).astype(jnp.bfloat16)
    return result.reshape(steps, block_requests, -1)


def solution(mesh):
    in_specs = (
        P(None, "gy", "gx"),
        P("gx", "gy"),
        P("gx", None),
        P("gy", "gx"),
        P(("gx", "gy"), None, None),
        P(("gx", "gy")),
    )
    out_specs = P(None, "gy", "gx")
    return jax.shard_map(
        per_device, mesh=mesh, in_specs=in_specs, out_specs=out_specs, check_vma=False
    )
```
